512 devices in a mesh: layer: 8 (over y_hi, core), ex: 64 (over x, y_lo, z).
Axes of the slice: x: 4, y: 8 (y_hi: 4, y_lo: 2; y = y_hi * 2 + y_lo), z: 8, core: 2. Of those that a mesh axis runs over, the one named last changes fastest.
Arguments:
- acts: bfloat16 [8, 12288, 8192], P('layer', 'ex'), may hold values from -6 to 6
- out_grads: bfloat16 [8, 12288, 1024], P('layer', 'ex'), may hold values from -6 to 6
- proj_in: bfloat16 [8, 64, 8192], P('layer'), may hold values from -0.0625 to 0.0625
- proj_out: bfloat16 [8, 64, 1024], P('layer'), may hold values from -0.1875 to 0.1875
- segment_ids: int32 [64, 192], P('ex'), may hold values from 0 to 47, never falling along the last dimension, each value on 1 to 8 neighbouring positions
Outputs:
- kernel: float32 [3072, 3072], P('ex', 'layer')
The draws below stay inside these ranges and needn't reach their ends.
Inputs may be any that keep to these rules, and one draw needn't show every extreme that they name: `segment_ids`: in each row the ids never fall, and every example of the block owns 1 to 8 consecutive tokens; some example owns exactly 8.
All inputs are finite; a program needn't handle non-finite values.
Results may differ from the reference program's by a relative error of at most 0.00037.
Values may be sent and summed in bfloat16 or wider, within the bound.
A program may use at most 64 MiB of HBM per device.

```python
import math
import jax
import jax.numpy as jnp
import numpy as np
from jax import lax

D = 8192
F = 1024
KIN = 64
KOUT = 64
EX_DEV = 48
TOK_DEV = 192
LAYERS = 8
EXAMPLES = 3072
TOKENS = 12288
N_EX = 64


def draw_acts(key, part):
    key = jax.random.fold_in(key, 11)
    first, second = jax.random.split(key, 2)
    common = jax.random.normal(first, (LAYERS, 1, D), jnp.float32)
    values = 0.6 * common + jax.random.normal(second, (LAYERS, TOKENS, D), jnp.float32)
    return jnp.clip(values, -6.0, 6.0).astype(jnp.bfloat16)


def draw_out_grads(key, part):
    key = jax.random.fold_in(key, 23)
    first, second = jax.random.split(key, 2)
    common = jax.random.normal(first, (LAYERS, 1, F), jnp.float32)
    values = 0.6 * common + jax.random.normal(second, (LAYERS, TOKENS, F), jnp.float32)
    return jnp.clip(values, -6.0, 6.0).astype(jnp.bfloat16)


def block_scale(stream_key, extent, pieces, least, top_value):
    level, own = 1.0, jax.random.fold_in(stream_key, 6)
    for dim, blocks in pieces:
        steps = jnp.exp(jax.random.uniform(jax.random.fold_in(own, dim), (blocks,), jnp.float32, least / len(pieces), top_value / len(pieces)))
        level = level * jnp.repeat(steps, extent[dim] // blocks).reshape([-1 if axis == dim else 1 for axis in range(len(extent))])
    return level


def length_profile(number_of, total, reach, lean):
    weights = [(1 << 20) // math.isqrt(standing ** lean) + 1 for standing in range(2, number_of + 1)]
    surplus, holding = total - reach - (number_of - 1), [1] * (number_of - 1)
    while surplus > 0:
        candidates = [i for i in range(number_of - 1) if holding[i] < reach]
        whole, left = sum([weights[i] for i in candidates]), surplus
        for i in candidates:
            addition = min(reach - holding[i], max(1, left * weights[i] // whole), surplus)
            holding[i] = holding[i] + addition
            surplus = surplus - addition
    return np.array([reach] + holding)


def uneven(rng, count, total, most, slope):
    if count == 2:
        one = jax.random.randint(rng, (), max(1, total - most), min(most, total - 1) + 1)
        return jnp.stack([one, total - one])
    tallies = jnp.asarray(length_profile(count, total, most, slope), jnp.int32)
    couples = (count - 1) // 2
    source_of, sink = tallies[1:1 + 2 * couples:2], tallies[2:2 + 2 * couples:2]
    room = jnp.minimum(source_of - 1, most - sink)
    moved = jax.random.randint(jax.random.fold_in(rng, 1), (couples,), 0, 1 << 20) % (room + 1)
    tallies = tallies.at[1:1 + 2 * couples:2].set(source_of - moved).at[2:2 + 2 * couples:2].set(sink + moved)
    return tallies[jax.random.permutation(jax.random.fold_in(rng, 2), count)]


def bell_draw(key, extent, deviation, most, cuts=(), held_as=jnp.bfloat16):
    entries = deviation * jax.random.normal(key, extent, jnp.float32)
    if cuts:
        entries = entries * block_scale(key, extent, cuts, -0.22, 0.18)
    return jnp.clip(entries, -most, most).astype(held_as)


def setup_inputs(seed: int = 0) -> dict:
    seeds = jax.random.split(jax.random.key(seed), 6)
    return {
        "acts": draw_acts(jax.random.fold_in(seeds[5], 71), 0),
        "out_grads": draw_out_grads(jax.random.fold_in(seeds[5], 71), 0),
        "proj_in": bell_draw(seeds[2], (LAYERS, KIN, D), D ** -0.5, 0.0625, ((0, 8),)),
        "proj_out": bell_draw(seeds[3], (LAYERS, KOUT, F), F ** -0.5, 0.1875, ((0, 8),)),
        "segment_ids": jax.vmap(lambda own: jnp.searchsorted(jnp.cumsum(uneven(own, EX_DEV, TOK_DEV, 8, 2)), jnp.arange(TOK_DEV), side="right"))(jax.random.split(seeds[4], N_EX)).reshape((N_EX, TOK_DEV)).astype(jnp.int32),
    }


def form_grads(onehot, u_block, v_block):
    tok = u_block.shape[0]
    count = onehot.shape[1]
    spread = (onehot[:, :, None] * u_block[:, None, :]).reshape(tok, count * KOUT)
    built = lax.dot_general(spread, v_block, (((0,), (0,)), ((), ())), preferred_element_type=jnp.float32)
    return built.reshape(count, KOUT * KIN).astype(jnp.bfloat16)


def reference(acts, out_grads, proj_in, proj_out, segment_ids):
    labels = jnp.arange(EX_DEV, dtype=jnp.int32)
    onehot = (segment_ids[:, :, None] == labels[None, None, :]).astype(jnp.bfloat16)
    kernel = jnp.zeros((EXAMPLES, EXAMPLES), jnp.float32)
    for layer in range(LAYERS):
        v_all = lax.dot_general(acts[layer], proj_in[layer], (((1,), (1,)), ((), ())), preferred_element_type=jnp.float32).astype(jnp.bfloat16)
        u_all = lax.dot_general(out_grads[layer], proj_out[layer], (((1,), (1,)), ((), ())), preferred_element_type=jnp.float32).astype(jnp.bfloat16)
        u_blocks = u_all.reshape(N_EX, TOK_DEV, KOUT)
        v_blocks = v_all.reshape(N_EX, TOK_DEV, KIN)

        def one_block(items):
            return form_grads(items[0], items[1], items[2])

        grads = lax.map(one_block, (onehot, u_blocks, v_blocks)).reshape(EXAMPLES, KOUT * KIN)
        kernel = kernel + jnp.dot(grads, grads.T, preferred_element_type=jnp.float32)
    return kernel * (1.0 / (2 * LAYERS * KIN * KOUT))
```

```python
import jax
import jax.numpy as jnp
from jax import lax
from jax.experimental import pallas as pl
from jax.experimental.pallas import tpu as pltpu
from jax.sharding import PartitionSpec as P

MESH = pl.DeviceIdType.MESH
BF = jnp.bfloat16
F32 = jnp.float32

EX = 48
TOK = 192
SIDE = 8
HALF = SIDE // 2
HEAD = 16
GTOK = HALF * TOK
GEX = HALF * EX
CHUNKS = 4


def dot_t(a, b):
    return lax.dot_general(a, b, (((1,), (1,)), ((), ())), preferred_element_type=F32)


def dot_n(a, b):
    return lax.dot_general(a, b, (((1,), (0,)), ((), ())), preferred_element_type=F32)


def split(x):
    hi = x.astype(BF)
    return hi, (x - hi.astype(F32)).astype(BF)


def kernel(
    acts, outg, pin, pout, seg, out,
    ab, gb, pib, pob, segb,
    rows, cols, rg, cu, cv, ohr, ohc, tbuf, tile, sib, red,
    in_sem, row_s, row_r, col_s, col_r, sib_s, sib_r, red_s, red_r,
):
    layer = lax.axis_index("layer")
    ex = lax.axis_index("ex")
    core = lax.rem(layer, 2)
    pair = layer // 2
    p = ex // SIDE
    q = lax.rem(ex, SIDE)
    kin = pin.shape[1]
    depth = acts.shape[2]
    piece = depth // CHUNKS

    loads = []

    def load(src, dst):
        copy = pltpu.make_async_copy(src, dst, in_sem.at[len(loads)])
        copy.start()
        loads.append(copy)

    for k in range(CHUNKS):
        at = pl.ds(k * piece, piece)
        load(pin.at[0, :, at], pib.at[:, at])
        load(acts.at[0, :, at], ab.at[:, at])
    load(pout.at[0], pob)
    load(outg.at[0], gb)
    load(seg, segb)

    row_peer = [(layer, lax.rem(p + d, SIDE) * SIDE + q) for d in range(1, SIDE)]
    col_peer = [(layer, p * SIDE + lax.rem(q + d, SIDE)) for d in range(1, SIDE)]
    other = (layer + 1 - 2 * core, ex)
    target = [(p, lax.rem(p + 4 * core + j, SIDE) * SIDE + q) for j in range(HALF)]
    part = lax.rem(p - layer + SIDE, SIDE) // HALF
    source = [(2 * y + part, layer * SIDE + q) for y in range(HALF)]
    to_self = jnp.logical_and(layer == p, core == 0)

    barrier = pltpu.get_barrier_semaphore()
    for device in row_peer + col_peer + [other]:
        pl.semaphore_signal(barrier, inc=1, device_id=device, device_id_type=MESH)
    for y in range(HALF):

        @pl.when(jnp.logical_not(jnp.logical_and(to_self, pair == y)))
        def _():
            pl.semaphore_signal(barrier, inc=1, device_id=source[y], device_id_type=MESH)

    loads[-1].wait()
    labels = segb[...].astype(F32)
    tail = labels[:, 128:TOK]
    low = labels[:, 0:128]
    line = lax.broadcasted_iota(jnp.int32, (HEAD, 128), 0)
    head = jnp.where(line == 0, low, jnp.concatenate([tail, tail], axis=1)).astype(BF)
    own_row = lax.rem(HALF + 4 * core, SIDE)
    loads[-3].wait()
    loads[-2].wait()
    u = dot_t(gb[...], pob[...])
    v = jnp.zeros((TOK, kin), F32)
    for k in range(CHUNKS):
        loads[2 * k].wait()
        loads[2 * k + 1].wait()
        at = pl.ds(k * piece, piece)
        v = v + dot_t(ab[:, at], pib[:, at])
    own = jnp.concatenate([u, v], axis=1).astype(BF)
    cols[1, 0:HEAD] = head
    cols[1, HEAD:] = own
    pl.semaphore_wait(barrier, 2 * (SIDE - 1) + 1 + HALF - to_self.astype(jnp.int32))

    row_copy, col_copy = [], []
    for d in range(1, SIDE):
        slot = (1 - d) % SIDE
        copy = pltpu.make_async_remote_copy(
            cols.at[1], cols.at[slot], col_s.at[d - 1], col_r.at[slot],
            device_id=col_peer[d - 1], device_id_type=MESH,
        )
        copy.start()
        col_copy.append(copy)
        slot = lax.rem(12 - d + 4 * core, SIDE)
        copy = pltpu.make_async_remote_copy(
            cols.at[1], rows.at[slot], row_s.at[d - 1], row_r.at[slot],
            device_id=row_peer[d - 1], device_id_type=MESH,
        )
        copy.start()
        row_copy.append(copy)
    rows[own_row] = cols[1]

    lane = lax.broadcasted_iota(jnp.int32, (TOK, 128), 1)
    left = lane < kin
    small = lax.broadcasted_iota(jnp.int32, (1, 128), 1) < TOK - 128
    spot = lax.broadcasted_iota(jnp.int32, (GEX, 128), 0).astype(F32)
    none = jnp.zeros((), BF)

    def place(dst, j, x):
        dst[j * 128 : (j + 1) * 128] = x[0:128]
        dst[HALF * 128 + j * 64 : HALF * 128 + (j + 1) * 64] = x[128:TOK]

    def onehot(dst, blocks):
        heads = [b[0:HEAD].astype(F32) for b in blocks]
        for j in range(HALF):
            mark = heads[j][0:1] + EX * j
            dst[:, j * 128 : (j + 1) * 128] = jnp.where(spot == mark, 1.0, 0.0).astype(BF)
        for m in range(HALF // 2):
            mark = jnp.where(
                small, heads[2 * m][1:2] + EX * 2 * m, heads[2 * m + 1][1:2] + EX * (2 * m + 1)
            )
            at = HALF * 128 + m * 128
            dst[:, at : at + 128] = jnp.where(spot == mark, 1.0, 0.0).astype(BF)

    def take_rows(r):
        for j in range(HALF):
            s = r * HALF + j

            @pl.when(s != own_row)
            def _():
                pltpu.make_async_remote_copy(
                    cols.at[1], rows.at[s], row_s.at[0], row_r.at[s],
                    device_id=other, device_id_type=MESH,
                ).wait_recv()

        for j in range(HALF):
            place(rg.at[r], j, rows[r * HALF + j, HEAD:])
        onehot(ohr.at[r], [rows.at[r * HALF + j] for j in range(HALF)])

    def take_cols(g):
        for j in range(HALF):
            s = g * HALF + j
            if s != 1:
                pltpu.make_async_remote_copy(
                    cols.at[1], cols.at[s], col_s.at[0], col_r.at[s],
                    device_id=other, device_id_type=MESH,
                ).wait_recv()
            x = cols[s, HEAD:]
            place(cu.at[g], j, jnp.where(left, x, none))
            place(cv.at[g], j, jnp.where(left, none, x))
        onehot(ohc.at[g], [cols.at[g * HALF + j] for j in range(HALF)])

    def quarter(r, g):
        for i in range(3):
            left_rows = rg[r, i * 256 : (i + 1) * 256]
            t = None
            for c in range(3):
                at = slice(c * 256, (c + 1) * 256)
                s = dot_t(left_rows, cu[g, at]) * dot_t(left_rows, cv[g, at])
                hi, lo = split(s)
                mark = ohc[g, :, at]
                step = dot_t(hi, mark) + dot_t(lo, mark)
                t = step if t is None else t + step
            tbuf[i * 256 : (i + 1) * 256] = t
        hi, lo = split(tbuf[...])
        tile[r, :, g * GEX : (g + 1) * GEX] = dot_n(ohr[r], hi) + dot_n(ohr[r], lo)

    take_rows(0)
    take_rows(1)
    take_cols(0)
    quarter(0, 0)
    quarter(1, 0)
    take_cols(1)
    quarter(0, 1)
    swap = pltpu.make_async_remote_copy(
        tile.at[0], sib, sib_s, sib_r, device_id=other, device_id_type=MESH
    )
    swap.start()
    quarter(1, 1)
    swap.wait_recv()
    sends = []
    for j in range(HALF):
        at = slice(j * EX, (j + 1) * EX)
        tile[1, at] = tile[1, at] + sib[at]
        copy = pltpu.make_async_remote_copy(
            tile.at[1, pl.ds(j * EX, EX)], red.at[pair], red_s.at[j], red_r.at[pair],
            device_id=target[j], device_id_type=MESH,
        )
        sends.append(copy)
        if j == 0:

            @pl.when(jnp.logical_not(to_self))
            def _():
                copy.start()

            @pl.when(to_self)
            def _():
                red[pair] = tile[1, at]
        else:
            copy.start()
    for y in range(HALF):

        @pl.when(jnp.logical_not(jnp.logical_and(to_self, pair == y)))
        def _():
            pltpu.make_async_remote_copy(
                tile.at[1, pl.ds(0, EX)], red.at[y], red_s.at[0], red_r.at[y],
                device_id=other, device_id_type=MESH,
            ).wait_recv()

    total = (red[0] + red[1]) + (red[2] + red[3])
    out[...] = pltpu.roll(total, lax.rem(q + SIDE - 1, SIDE) * EX, 1)

    for copy in row_copy + col_copy + [swap] + sends[1:]:
        copy.wait_send()

    @pl.when(jnp.logical_not(to_self))
    def _():
        sends[0].wait_send()


def per_device(acts, out_grads, proj_in, proj_out, segment_ids):
    kin, depth = proj_in.shape[1:]
    kout, width = proj_out.shape[1:]
    layers = lax.axis_size("layer")
    sem = pltpu.SemaphoreType.DMA
    total = pl.pallas_call(
        kernel,
        name="tile",
        out_shape=jax.ShapeDtypeStruct((EX, SIDE * EX), F32),
        in_specs=[pl.BlockSpec(memory_space=pl.ANY)] * 5,
        out_specs=pl.BlockSpec(memory_space=pltpu.VMEM),
        scratch_shapes=[
            pltpu.VMEM((TOK, depth), BF),
            pltpu.VMEM((TOK, width), BF),
            pltpu.VMEM((kin, depth), BF),
            pltpu.VMEM((kout, width), BF),
            pltpu.VMEM((1, TOK), jnp.int32),
            pltpu.VMEM((SIDE, HEAD + TOK, kin + kout), BF),
            pltpu.VMEM((SIDE, HEAD + TOK, kin + kout), BF),
            pltpu.VMEM((2, GTOK, kin + kout), BF),
            pltpu.VMEM((2, GTOK, kin + kout), BF),
            pltpu.VMEM((2, GTOK, kin + kout), BF),
            pltpu.VMEM((2, GEX, GTOK), BF),
            pltpu.VMEM((2, GEX, GTOK), BF),
            pltpu.VMEM((GTOK, GEX), F32),
            pltpu.VMEM((2, GEX, 2 * GEX), F32),
            pltpu.VMEM((GEX, 2 * GEX), F32),
            pltpu.VMEM((HALF, EX, 2 * GEX), F32),
            sem((2 * CHUNKS + 3,)),
            sem((SIDE - 1,)),
            sem((SIDE,)),
            sem((SIDE - 1,)),
            sem((SIDE,)),
            sem,
            sem,
            sem((HALF,)),
            sem((HALF,)),
        ],
        compiler_params=pltpu.CompilerParams(
            collective_id=0, has_side_effects=True, vmem_limit_bytes=60 << 20
        ),
    )(acts, out_grads, proj_in, proj_out, segment_ids)
    return total * (1.0 / (2 * layers * kin * kout))


def solution(mesh):
    in_specs = (
        P("layer", "ex", None),
        P("layer", "ex", None),
        P("layer", None, None),
        P("layer", None, None),
        P("ex", None),
    )
    out_specs = P("ex", "layer")
    return jax.shard_map(
        per_device, mesh=mesh, in_specs=in_specs, out_specs=out_specs, check_vma=False
    )
```

```python
import jax
import jax.numpy as jnp
from jax import lax
from jax.experimental import pallas as pl
from jax.experimental.pallas import tpu as pltpu
from jax.sharding import PartitionSpec as P

MESH = pl.DeviceIdType.MESH
BF = jnp.bfloat16
F32 = jnp.float32

EX = 48
TOK = 192
SIDE = 8
HALF = SIDE // 2
HEAD = 16
GTOK = HALF * TOK
GEX = HALF * EX
CHUNKS = 4


def dot_t(a, b):
    return lax.dot_general(a, b, (((1,), (1,)), ((), ())), preferred_element_type=F32)


def dot_n(a, b):
    return lax.dot_general(a, b, (((1,), (0,)), ((), ())), preferred_element_type=F32)


def split(x):
    hi = x.astype(BF)
    return hi, (x - hi.astype(F32)).astype(BF)


def kernel(
    acts, outg, pin, pout, seg, out,
    ab, gb, pib, pob, segb,
    across, along, rg, cu, cv, ohr, ohc, tbuf, tile, sib, stage, red,
    in_sem, across_s, across_r, along_s, along_r, sib_s, sib_r, red_s, red_r,
):
    layer = lax.axis_index("layer")
    ex = lax.axis_index("ex")
    core = lax.rem(layer, 2)
    pair = layer // 2
    p = ex // SIDE
    q = lax.rem(ex, SIDE)
    kin = pin.shape[1]
    depth = acts.shape[2]
    piece = depth // CHUNKS

    loads = []

    def load(src, dst):
        copy = pltpu.make_async_copy(src, dst, in_sem.at[len(loads)])
        copy.start()
        loads.append(copy)

    for k in range(CHUNKS):
        at = pl.ds(k * piece, piece)
        load(pin.at[0, :, at], pib.at[:, at])
        load(acts.at[0, :, at], ab.at[:, at])
    load(pout.at[0], pob)
    load(outg.at[0], gb)
    load(seg, segb)

    across_peer = [(layer, lax.rem(p + d, SIDE) * SIDE + q) for d in range(1, SIDE)]
    along_peer = [(layer, p * SIDE + lax.rem(q + d, SIDE)) for d in range(1, SIDE)]
    other = (layer + 1 - 2 * core, ex)

    def owner(k, d):
        return (2 * lax.rem(pair + k, HALF) + core, p * SIDE + lax.rem(q + d, SIDE))

    barrier = pltpu.get_barrier_semaphore()
    greet = across_peer + along_peer + [other]
    greet += [owner(k, d) for k in range(1, HALF) for d in range(SIDE)]
    for device in greet:
        pl.semaphore_signal(barrier, inc=1, device_id=device, device_id_type=MESH)

    loads[-1].wait()
    labels = segb[...].astype(F32)
    tail = labels[:, 128:TOK]
    low = labels[:, 0:128]
    line = lax.broadcasted_iota(jnp.int32, (HEAD, 128), 0)
    head = jnp.where(line == 0, low, jnp.concatenate([tail, tail], axis=1)).astype(BF)
    loads[-3].wait()
    loads[-2].wait()
    u = dot_t(gb[...], pob[...])
    v = jnp.zeros((TOK, kin), F32)
    for k in range(CHUNKS):
        loads[2 * k].wait()
        loads[2 * k + 1].wait()
        at = pl.ds(k * piece, piece)
        v = v + dot_t(ab[:, at], pib[:, at])
    own = jnp.concatenate([u, v], axis=1).astype(BF)
    along[1, 0:HEAD] = head
    along[1, HEAD:] = own
    pl.semaphore_wait(barrier, len(greet))

    mine = HALF * (1 - lax.rem(lax.rem(p, 2) + core, 2)) + p // 2
    sent = []
    for d in (1, 7, 2, 6, 3, 5, 4):
        slot = (1 - d) % SIDE
        copy = pltpu.make_async_remote_copy(
            along.at[1], along.at[slot], along_s.at[d - 1], along_r.at[slot],
            device_id=along_peer[d - 1], device_id_type=MESH,
        )
        copy.start()
        sent.append(copy)
        copy = pltpu.make_async_remote_copy(
            along.at[1], across.at[mine], across_s.at[d - 1], across_r.at[mine],
            device_id=across_peer[d - 1], device_id_type=MESH,
        )
        copy.start()
        sent.append(copy)
    across[mine] = along[1]

    def arrived(dst, sem):
        pltpu.make_async_remote_copy(
            dst, dst, sib_s.at[0], sem, device_id=other, device_id_type=MESH
        ).wait_recv()

    lane = lax.broadcasted_iota(jnp.int32, (TOK, 128), 1)
    left = lane < kin
    small = lax.broadcasted_iota(jnp.int32, (1, 128), 1) < TOK - 128
    spot = lax.broadcasted_iota(jnp.int32, (GEX, 128), 0).astype(F32)
    none = jnp.zeros((), BF)

    def place(dst, j, x):
        dst[j * 128 : (j + 1) * 128] = x[0:128]
        dst[HALF * 128 + j * 64 : HALF * 128 + (j + 1) * 64] = x[128:TOK]

    def onehot(dst, blocks):
        heads = [b[0:HEAD].astype(F32) for b in blocks]
        for j in range(HALF):
            mark = heads[j][0:1] + EX * j
            dst[:, j * 128 : (j + 1) * 128] = jnp.where(spot == mark, 1.0, 0.0).astype(BF)
        for m in range(HALF // 2):
            mark = jnp.where(
                small, heads[2 * m][1:2] + EX * 2 * m, heads[2 * m + 1][1:2] + EX * (2 * m + 1)
            )
            at = HALF * 128 + m * 128
            dst[:, at : at + 128] = jnp.where(spot == mark, 1.0, 0.0).astype(BF)

    def take_across(g):
        for s in range(g * HALF, (g + 1) * HALF):

            @pl.when(s != mine)
            def _():
                arrived(across.at[s], across_r.at[s])

        for j in range(HALF):
            x = across[g * HALF + j, HEAD:]
            place(cu.at[g], j, jnp.where(left, x, none))
            place(cv.at[g], j, jnp.where(left, none, x))
        onehot(ohc.at[g], [across.at[g * HALF + j] for j in range(HALF)])

    def take_along(h):
        for s in range(h * HALF, (h + 1) * HALF):
            if s != 1:
                arrived(along.at[s], along_r.at[s])
            place(rg.at[h], s % HALF, along[s, HEAD:])
        onehot(ohr.at[h], [along.at[h * HALF + j] for j in range(HALF)])

    def quarter(g, h):
        for i in range(3):
            left_rows = rg[h, i * 256 : (i + 1) * 256]
            t = None
            for c in range(3):
                at = slice(c * 256, (c + 1) * 256)
                s = dot_t(left_rows, cu[g, at]) * dot_t(left_rows, cv[g, at])
                hi, lo = split(s)
                mark = ohc[g, :, at]
                step = dot_t(hi, mark) + dot_t(lo, mark)
                t = step if t is None else t + step
            tbuf[i * 256 : (i + 1) * 256] = t
        hi, lo = split(tbuf[...])
        tile[g, h] = dot_n(ohr[h], hi) + dot_n(ohr[h], lo)

    def swap(h):
        copy = pltpu.make_async_remote_copy(
            tile.at[0, h], sib.at[h], sib_s.at[h], sib_r.at[h],
            device_id=other, device_id_type=MESH,
        )
        copy.start()
        sent.append(copy)

    def deliver(h):
        arrived(sib.at[h], sib_r.at[h])
        for j in range(HALF):
            s = h * HALF + j
            d = (s - 1) % SIDE
            for x in range(HALF):
                e = x * EX
                rows = slice(j * EX, (j + 1) * EX)
                both = tile[1, h, rows, e : e + EX] + sib[h, rows, e : e + EX]
                stage[s, x, :, 0 : 2 * EX] = jnp.concatenate(
                    [both[0 : EX // 2], both[EX // 2 :]], axis=1
                )
            for k in range(HALF):
                x = lax.rem(pair + k, HALF)
                if k == 0 and d == 0:
                    red[pair, q] = stage[s, x]
                    continue
                copy = pltpu.make_async_remote_copy(
                    stage.at[s, x], red.at[pair, q], red_s.at[s, k], red_r.at[pair, q],
                    device_id=owner(k, d), device_id_type=MESH,
                )
                copy.start()
                sent.append(copy)

    take_across(0)
    take_along(0)
    quarter(0, 0)
    swap(0)
    take_across(1)
    quarter(1, 0)
    deliver(0)
    take_along(1)
    quarter(0, 1)
    swap(1)
    quarter(1, 1)
    deliver(1)

    for d in (0, 7, 1, 6, 2, 5, 3, 4):
        for k in range(HALF):
            if k or d:
                y, z = lax.rem(pair + k, HALF), lax.rem(q + d, SIDE)
                arrived(red.at[y, z], red_r.at[y, z])
    for z in range(SIDE):
        total = (red[0, z] + red[1, z]) + (red[2, z] + red[3, z])
        out[0 : EX // 2, z * EX : (z + 1) * EX] = total[:, 0:EX]
        out[EX // 2 : EX, z * EX : (z + 1) * EX] = total[:, EX : 2 * EX]

    for copy in sent:
        copy.wait_send()


def per_device(acts, out_grads, proj_in, proj_out, segment_ids):
    kin, depth = proj_in.shape[1:]
    kout, width = proj_out.shape[1:]
    layers = lax.axis_size("layer")
    sem = pltpu.SemaphoreType.DMA
    total = pl.pallas_call(
        kernel,
        name="tile",
        out_shape=jax.ShapeDtypeStruct((EX, SIDE * EX), F32),
        in_specs=[pl.BlockSpec(memory_space=pl.ANY)] * 5,
        out_specs=pl.BlockSpec(memory_space=pltpu.VMEM),
        scratch_shapes=[
            pltpu.VMEM((TOK, depth), BF),
            pltpu.VMEM((TOK, width), BF),
            pltpu.VMEM((kin, depth), BF),
            pltpu.VMEM((kout, width), BF),
            pltpu.VMEM((1, TOK), jnp.int32),
            pltpu.VMEM((SIDE, HEAD + TOK, kin + kout), BF),
            pltpu.VMEM((SIDE, HEAD + TOK, kin + kout), BF),
            pltpu.VMEM((2, GTOK, kin + kout), BF),
            pltpu.VMEM((2, GTOK, kin + kout), BF),
            pltpu.VMEM((2, GTOK, kin + kout), BF),
            pltpu.VMEM((2, GEX, GTOK), BF),
            pltpu.VMEM((2, GEX, GTOK), BF),
            pltpu.VMEM((GTOK, GEX), F32),
            pltpu.VMEM((2, 2, GEX, GEX), F32),
            pltpu.VMEM((2, GEX, GEX), F32),
            pltpu.VMEM((SIDE, HALF, EX // 2, 128), F32),
            pltpu.VMEM((HALF, SIDE, EX // 2, 128), F32),
            sem((2 * CHUNKS + 3,)),
            sem((SIDE - 1,)),
            sem((SIDE,)),
            sem((SIDE - 1,)),
            sem((SIDE,)),
            sem((2,)),
            sem((2,)),
            sem((SIDE, HALF)),
            sem((HALF, SIDE)),
        ],
        compiler_params=pltpu.CompilerParams(
            collective_id=0, has_side_effects=True, vmem_limit_bytes=60 << 20
        ),
    )(acts, out_grads, proj_in, proj_out, segment_ids)
    return total * (1.0 / (2 * layers * kin * kout))


def solution(mesh):
    in_specs = (
        P("layer", "ex", None),
        P("layer", "ex", None),
        P("layer", None, None),
        P("layer", None, None),
        P("ex", None),
    )
    out_specs = P("ex", "layer")
    return jax.shard_map(
        per_device, mesh=mesh, in_specs=in_specs, out_specs=out_specs, check_vma=False
    )
```

```python
import jax
import jax.numpy as jnp
from jax import lax
from jax.experimental import pallas as pl
from jax.experimental.pallas import tpu as pltpu
from jax.sharding import PartitionSpec as P

MESH = pl.DeviceIdType.MESH
BF = jnp.bfloat16
F32 = jnp.float32

EX = 48
TOK = 192
SIDE = 8
HALF = SIDE // 2
HEAD = 16
GTOK = HALF * TOK
GEX = HALF * EX
UNITS = ((1, 0, 2), (3, 7), (5, 4), (6,))
CODE = 32767.0
CHUNKS = 4


def dot_t(a, b):
    return lax.dot_general(a, b, (((1,), (1,)), ((), ())), preferred_element_type=F32)


def dot_n(a, b):
    return lax.dot_general(a, b, (((1,), (0,)), ((), ())), preferred_element_type=F32)


def split(x):
    hi = x.astype(BF)
    return hi, (x - hi.astype(F32)).astype(BF)


def kernel(
    acts, outg, pin, pout, seg, out,
    ab, gb, pib, pob, segb,
    across, along, cu, cv, ohc, tile, sib, stage, red, acc,
    in_sem, across_s, across_r, along_s, along_r, sib_s, sib_r, red_s, red_r,
):
    layer = lax.axis_index("layer")
    ex = lax.axis_index("ex")
    core = lax.rem(layer, 2)
    pair = layer // 2
    p = ex // SIDE
    q = lax.rem(ex, SIDE)
    kin = pin.shape[1]
    depth = acts.shape[2]
    piece = depth // CHUNKS

    loads = []

    def load(src, dst):
        copy = pltpu.make_async_copy(src, dst, in_sem.at[len(loads)])
        copy.start()
        loads.append(copy)

    for k in range(CHUNKS):
        at = pl.ds(k * piece, piece)
        load(pin.at[0, :, at], pib.at[:, at])
        load(acts.at[0, :, at], ab.at[:, at])
    load(pout.at[0], pob)
    load(outg.at[0], gb)
    load(seg, segb)

    px, py = p // 2, lax.rem(p, 2)

    def across_device(d, e):
        return (layer, (2 * lax.rem(px + d, HALF) + lax.rem(py + e, 2)) * SIDE + q)

    def along_device(d):
        return (layer, p * SIDE + lax.rem(q + d, SIDE))

    other = (layer + 1 - 2 * core, ex)

    def owner(k, d):
        return (2 * lax.rem(pair + k, HALF) + core, p * SIDE + lax.rem(q + d, SIDE))

    barrier = pltpu.get_barrier_semaphore()
    greet = [along_device(d) for d in range(1, SIDE)] + [other]
    greet += [across_device(d, e) for e in range(2) for d in range(HALF) if d or e]
    greet += [owner(k, d) for k in range(1, HALF) for d in range(SIDE)]
    for device in greet:
        pl.semaphore_signal(barrier, inc=1, device_id=device, device_id_type=MESH)

    loads[-1].wait()
    labels = segb[...].astype(F32)
    tail = labels[:, 128:TOK]
    low = labels[:, 0:128]
    line = lax.broadcasted_iota(jnp.int32, (HEAD, 128), 0)
    head = jnp.where(line == 0, low, jnp.concatenate([tail, tail], axis=1)).astype(BF)
    loads[-3].wait()
    loads[-2].wait()
    u = dot_t(gb[...], pob[...])
    v = jnp.zeros((TOK, kin), F32)
    for k in range(CHUNKS):
        loads[2 * k].wait()
        loads[2 * k + 1].wait()
        at = pl.ds(k * piece, piece)
        v = v + dot_t(ab[:, at], pib[:, at])
    own = jnp.concatenate([u, v], axis=1).astype(BF)
    along[1, 0:HEAD] = head
    along[1, HEAD:] = own
    pl.semaphore_wait(barrier, len(greet))

    sent = []

    def send(src, dst, send_sem, recv_sem, device):
        copy = pltpu.make_async_remote_copy(
            src, dst, send_sem, recv_sem, device_id=device, device_id_type=MESH
        )
        copy.start()
        sent.append(copy)

    def send_across(d, e):
        to = HALF * e + px
        sem = across_s.at[HALF * e + d]
        send(along.at[1], across.at[to], sem, across_r.at[to], across_device(d, e))

    def send_along(d):
        to = (1 - d) % SIDE
        send(along.at[1], along.at[to], along_s.at[d], along_r.at[to], along_device(d))

    def pass_on(src, to, d, sem, at):
        rows = pl.ds(*at)
        send(
            along.at[src, rows], along.at[to, rows], along_s.at[sem + SIDE], along_r.at[sem],
            along_device(d),
        )

    for d in (2, 6):
        send_along(d)
    for d in (1, 3, 2):
        send_across(d, 0)
    for d in (1, 7):
        send_along(d)
    for d in (0, 1, 3, 2):
        send_across(d, 1)
    across[px] = along[1]

    def arrived(dst, sem):
        pltpu.make_async_remote_copy(
            dst, dst, sib_s.at[0], sem, device_id=other, device_id_type=MESH
        ).wait_recv()

    lane = lax.broadcasted_iota(jnp.int32, (TOK, 128), 1)
    left = lane < kin
    small = lax.broadcasted_iota(jnp.int32, (1, 128), 1) < TOK - 128
    spot = lax.broadcasted_iota(jnp.int32, (GEX, 128), 0).astype(F32)
    none = jnp.zeros((), BF)
    line48 = lax.broadcasted_iota(jnp.int32, (EX, TOK), 0).astype(F32)

    def place(dst, j, x):
        dst[j * 128 : (j + 1) * 128] = x[0:128]
        dst[HALF * 128 + j * 64 : HALF * 128 + (j + 1) * 64] = x[128:TOK]

    def onehot(dst, blocks):
        heads = [b[0:HEAD].astype(F32) for b in blocks]
        for j in range(HALF):
            mark = heads[j][0:1] + EX * j
            dst[:, j * 128 : (j + 1) * 128] = jnp.where(spot == mark, 1.0, 0.0).astype(BF)
        for m in range(HALF // 2):
            mark = jnp.where(
                small, heads[2 * m][1:2] + EX * 2 * m, heads[2 * m + 1][1:2] + EX * (2 * m + 1)
            )
            at = HALF * 128 + m * 128
            dst[:, at : at + 128] = jnp.where(spot == mark, 1.0, 0.0).astype(BF)

    def take_across(g):
        for d in range(HALF):
            if d or g:
                at = g * HALF + lax.rem(px + d, HALF)
                arrived(across.at[at], across_r.at[at])
        for j in range(HALF):
            x = across[g * HALF + j, HEAD:]
            place(cu.at[g], j, jnp.where(left, x, none))
            place(cv.at[g], j, jnp.where(left, none, x))
        onehot(ohc.at[g], [across.at[g * HALF + j] for j in range(HALF)])

    def take_along(unit):
        for s in unit:
            if s in (0, 2, 4, 6):
                arrived(along.at[s], along_r.at[s])
            elif s == 5:
                arrived(along.at[5, 0 : HEAD + TOK // 2], along_r.at[5])
                arrived(along.at[5, HEAD + TOK // 2 :], along_r.at[8])

    def strip(g, unit):
        left_rows = jnp.concatenate([along[s, HEAD:] for s in unit], axis=0)
        t = None
        for c in range(GTOK // 256):
            at = slice(c * 256, (c + 1) * 256)
            hi, lo = split(dot_t(left_rows, cu[g, at]) * dot_t(left_rows, cv[g, at]))
            mark = ohc[g, :, at]
            step = dot_t(hi, mark) + dot_t(lo, mark)
            t = step if t is None else t + step
        for i, s in enumerate(unit):
            marks = along[s, 0:HEAD].astype(F32)
            mark = jnp.concatenate([marks[0:1], marks[1:2, 0 : TOK - 128]], axis=1)
            mark = jnp.where(line48 == mark, 1.0, 0.0).astype(BF)
            hi, lo = split(t[i * TOK : (i + 1) * TOK])
            tile[g, s] = dot_n(mark, hi) + dot_n(mark, lo)

    keep = lax.rem(py + core, 2)
    give = 1 - keep

    def swap(unit):
        for s in unit:
            send(tile.at[give, s], sib.at[s], sib_s.at[s], sib_r.at[s], other)

    def deliver(unit):
        for s in unit:
            arrived(sib.at[s], sib_r.at[s])
            d = (s - 1) % SIDE
            both = tile[keep, s] + sib[s]
            size = jnp.abs(both)
            top = jnp.max(size, axis=(0, 1), keepdims=True)
            power = jnp.ceil(jnp.log2(jnp.maximum(top, 1e-30)) + 1e-4)
            code = (jnp.sqrt(size * jnp.exp2(-power)) * CODE + 0.5).astype(jnp.int32)
            code = jnp.where(both < 0, -code, code)
            word = code[0 : EX // 2] * 65536 + (code[EX // 2 :] & 65535)
            note = jnp.broadcast_to(power.astype(jnp.int32), (8, 128 - 2 * EX))
            for x in range(HALF):
                w = word[:, x * EX : (x + 1) * EX]
                stage[s, x, 0:8] = jnp.concatenate([w[0:8], w[8:16], note], axis=1)
                stage[s, x, 8:12] = jnp.concatenate([w[16:20], w[20:24], note[0:4]], axis=1)
            to = (1 - d) % SIDE
            for k in range(HALF):
                x = lax.rem(pair + k, HALF)
                if k == 0 and d == 0:
                    red[pair, to] = stage[s, x]
                else:
                    sem = red_r.at[pair, to]
                    send(stage.at[s, x], red.at[pair, to], red_s.at[s, k], sem, owner(k, d))

    arrived(along.at[7], along_r.at[7])
    pass_on(7, 6, 1, 6, (0, HEAD + TOK))
    pass_on(7, 5, 2, 5, (0, HEAD + TOK // 2))
    arrived(along.at[3], along_r.at[3])
    pass_on(3, 4, 7, 4, (0, HEAD + TOK))
    pass_on(3, 5, 6, 8, (HEAD + TOK // 2, TOK // 2))
    take_across(0)
    take_along(UNITS[0])
    strip(0, UNITS[0])
    take_across(1)
    strip(1, UNITS[0])
    swap(UNITS[0])
    for before, unit in zip(UNITS, UNITS[1:]):
        take_along(unit)
        strip(give, unit)
        strip(keep, unit)
        swap(unit)
        deliver(before)
    deliver(UNITS[-1])

    for s in (1, 0, 2, 7, 3, 6, 4, 5):
        sums = []
        for k in range(HALF):
            y = lax.rem(pair + k, HALF)
            if k or s != 1:
                arrived(red.at[y, s], red_r.at[y, s])
        for y in range(HALF):
            word = red[y, s]
            scale = jnp.exp2(word[:, 2 * EX : 2 * EX + 1].astype(F32)) * (1.0 / (CODE * CODE))
            for half in (word >> 16, (word << 16) >> 16):
                code = half.astype(F32)
                sums.append(code * jnp.abs(code) * scale)
        at = slice(s * EX, (s + 1) * EX)
        for h in range(2):
            part = (sums[h] + sums[2 + h]) + (sums[4 + h] + sums[6 + h])
            base = h * (EX // 2)
            acc[base : base + 8, at] = part[0:8, 0:EX]
            acc[base + 8 : base + 16, at] = part[0:8, EX : 2 * EX]
            acc[base + 16 : base + 20, at] = part[8:12, 0:EX]
            acc[base + 20 : base + 24, at] = part[8:12, EX : 2 * EX]
    out[...] = pltpu.roll(acc[...], lax.rem(q + SIDE - 1, SIDE) * EX, 1)

    for copy in sent:
        copy.wait_send()


def per_device(acts, out_grads, proj_in, proj_out, segment_ids):
    kin, depth = proj_in.shape[1:]
    kout, width = proj_out.shape[1:]
    layers = lax.axis_size("layer")
    sem = pltpu.SemaphoreType.DMA
    total = pl.pallas_call(
        kernel,
        name="tile",
        out_shape=jax.ShapeDtypeStruct((EX, SIDE * EX), F32),
        in_specs=[pl.BlockSpec(memory_space=pl.ANY)] * 5,
        out_specs=pl.BlockSpec(memory_space=pltpu.VMEM),
        scratch_shapes=[
            pltpu.VMEM((TOK, depth), BF),
            pltpu.VMEM((TOK, width), BF),
            pltpu.VMEM((kin, depth), BF),
            pltpu.VMEM((kout, width), BF),
            pltpu.VMEM((1, TOK), jnp.int32),
            pltpu.VMEM((SIDE, HEAD + TOK, kin + kout), BF),
            pltpu.VMEM((SIDE, HEAD + TOK, kin + kout), BF),
            pltpu.VMEM((2, GTOK, kin + kout), BF),
            pltpu.VMEM((2, GTOK, kin + kout), BF),
            pltpu.VMEM((2, GEX, GTOK), BF),
            pltpu.VMEM((2, SIDE, EX, GEX), F32),
            pltpu.VMEM((SIDE, EX, GEX), F32),
            pltpu.VMEM((SIDE, HALF, EX // 4, 128), jnp.int32),
            pltpu.VMEM((HALF, SIDE, EX // 4, 128), jnp.int32),
            pltpu.VMEM((EX, SIDE * EX), F32),
            sem((2 * CHUNKS + 3,)),
            sem((SIDE,)),
            sem((SIDE,)),
            sem((2 * SIDE + 1,)),
            sem((SIDE + 1,)),
            sem((SIDE,)),
            sem((SIDE,)),
            sem((SIDE, HALF)),
            sem((HALF, SIDE)),
        ],
        compiler_params=pltpu.CompilerParams(
            collective_id=0, has_side_effects=True, vmem_limit_bytes=60 << 20
        ),
    )(acts, out_grads, proj_in, proj_out, segment_ids)
    return total * (1.0 / (2 * layers * kin * kout))


def solution(mesh):
    in_specs = (
        P("layer", "ex", None),
        P("layer", "ex", None),
        P("layer", None, None),
        P("layer", None, None),
        P("ex", None),
    )
    out_specs = P("ex", "layer")
    return jax.shard_map(
        per_device, mesh=mesh, in_specs=in_specs, out_specs=out_specs, check_vma=False
    )
```

```python
import jax
import jax.numpy as jnp
from jax import lax
from jax.experimental import pallas as pl
from jax.experimental.pallas import tpu as pltpu
from jax.sharding import PartitionSpec as P

MESH = pl.DeviceIdType.MESH
BF = jnp.bfloat16
F32 = jnp.float32

EX = 48
TOK = 192
SIDE = 8
HALF = SIDE // 2
HEAD = 16
GTOK = HALF * TOK
GEX = HALF * EX
UNITS = ((1, 0, 2, 3, 7), (5, 4, 6))
CODE = 32767.0
CHUNKS = 4


def dot_t(a, b):
    return lax.dot_general(a, b, (((1,), (1,)), ((), ())), preferred_element_type=F32)


def dot_n(a, b):
    return lax.dot_general(a, b, (((1,), (0,)), ((), ())), preferred_element_type=F32)


def split(x):
    hi = x.astype(BF)
    return hi, (x - hi.astype(F32)).astype(BF)


def kernel(
    acts, outg, pin, pout, seg, out,
    ab, gb, pib, pob, segb,
    across, along, cu, cv, ohc, tile, stage, red, acc,
    in_sem, across_s, across_r, along_s, along_r, sib_s, sib_r, red_s, red_r, ready,
):
    layer = lax.axis_index("layer")
    ex = lax.axis_index("ex")
    core = lax.rem(layer, 2)
    pair = layer // 2
    p = ex // SIDE
    q = lax.rem(ex, SIDE)
    kin = pin.shape[1]
    depth = acts.shape[2]
    piece = depth // CHUNKS

    loads = []

    def load(src, dst):
        copy = pltpu.make_async_copy(src, dst, in_sem.at[len(loads)])
        copy.start()
        loads.append(copy)

    load(seg, segb)
    load(pout.at[0], pob)
    load(outg.at[0], gb)
    for k in range(CHUNKS):
        at = pl.ds(k * piece, piece)
        load(pin.at[0, :, at], pib.at[:, at])
        load(acts.at[0, :, at], ab.at[:, at])

    px, py = p // 2, lax.rem(p, 2)
    home = py == core

    def across_to(d, e):
        return (2 * pair + py, (2 * lax.rem(px + d, HALF) + lax.rem(py + e, 2)) * SIDE + q)

    def across_from(d, e):
        return (2 * pair + lax.rem(core + e, 2), (2 * lax.rem(px + d, HALF) + core) * SIDE + q)

    def along_device(d):
        return (layer, p * SIDE + lax.rem(q + d, SIDE))

    other = (layer + 1 - 2 * core, ex)

    def owner(k, d):
        return (2 * lax.rem(pair + k, HALF) + core, p * SIDE + lax.rem(q + d, SIDE))

    barrier = pltpu.get_barrier_semaphore()
    def signal(device):
        pl.semaphore_signal(barrier, inc=1, device_id=device, device_id_type=MESH)

    for d in range(1, SIDE):
        signal(along_device(d))
    signal(other)
    for e in range(2):
        for d in range(HALF):
            if d or e:
                signal(across_from(d, e))

    @pl.when(jnp.logical_not(home))
    def _():
        signal(across_from(0, 0))

    for k in range(1, HALF):
        signal(owner(k, 0))
    greeted = (SIDE - 1) + 1 + SIDE + (HALF - 1) - home.astype(jnp.int32)

    loads[0].wait()
    labels = segb[...].astype(F32)
    tail = labels[:, 128:TOK]
    low = labels[:, 0:128]
    line = lax.broadcasted_iota(jnp.int32, (HEAD, 128), 0)
    head = jnp.where(line == 0, low, jnp.concatenate([tail, tail], axis=1)).astype(BF)
    loads[1].wait()
    loads[2].wait()
    along[0, 1, 0:HEAD] = head
    u = dot_t(gb[...], pob[...])
    v = jnp.zeros((TOK, kin), F32)
    for k in range(CHUNKS):
        loads[3 + 2 * k].wait()
        loads[4 + 2 * k].wait()
        at = pl.ds(k * piece, piece)
        v = v + dot_t(ab[:, at], pib[:, at])
    own = jnp.concatenate([u, v], axis=1).astype(BF)
    along[0, 1, HEAD:] = own
    pl.semaphore_wait(barrier, greeted)
    for k in range(1, HALF):
        pl.semaphore_signal(ready, inc=1, device_id=owner(k, 0), device_id_type=MESH)

    sent = []

    def send(src, dst, send_sem, recv_sem, device):
        copy = pltpu.make_async_remote_copy(
            src, dst, send_sem, recv_sem, device_id=device, device_id_type=MESH
        )
        copy.start()
        sent.append(copy)

    mine = along.at[0]
    to_across = HALF * lax.rem(core + py, 2) + px

    def send_across(d, e):
        sem = across_s.at[HALF * e + d]
        send(mine.at[1], across.at[to_across], sem, across_r.at[to_across], across_to(d, e))

    def send_along(d):
        to = (1 - d) % SIDE
        send(mine.at[1], mine.at[to], along_s.at[d], along_r.at[to], along_device(d))

    def pass_on(src, to, d, sem, at):
        rows = pl.ds(*at)
        send(
            mine.at[src, rows], mine.at[to, rows], along_s.at[sem + SIDE], along_r.at[sem],
            along_device(d),
        )

    def share(s):
        send(mine.at[s], along.at[1, s], sib_s.at[s], sib_r.at[s], other)

    for d in (2, 6):
        send_along(d)
    for d in (1, 3, 2):
        send_across(d, 0)
    for d in (1, 7):
        send_along(d)
    for d in (0, 1, 3, 2):
        send_across(d, 1)
    share(1)
    to_core = pltpu.make_async_remote_copy(
        mine.at[1], across.at[to_across], across_s.at[0], across_r.at[to_across],
        device_id=other, device_id_type=MESH,
    )

    @pl.when(home)
    def _():
        across[px] = along[0, 1]

    @pl.when(jnp.logical_not(home))
    def _():
        to_core.start()

    def arrived(dst, sem):
        pltpu.make_async_remote_copy(
            dst, dst, sib_s.at[0], sem, device_id=other, device_id_type=MESH
        ).wait_recv()

    lane = lax.broadcasted_iota(jnp.int32, (TOK, 128), 1)
    left = lane < kin
    small = lax.broadcasted_iota(jnp.int32, (1, 128), 1) < TOK - 128
    spot = lax.broadcasted_iota(jnp.int32, (GEX, 128), 0).astype(F32)
    none = jnp.zeros((), BF)
    line48 = lax.broadcasted_iota(jnp.int32, (EX, TOK), 0).astype(F32)

    def place(dst, j, x):
        dst[j * 128 : (j + 1) * 128] = x[0:128]
        dst[HALF * 128 + j * 64 : HALF * 128 + (j + 1) * 64] = x[128:TOK]

    def onehot(dst, blocks):
        heads = [b[0:HEAD].astype(F32) for b in blocks]
        for j in range(HALF):
            mark = heads[j][0:1] + EX * j
            dst[:, j * 128 : (j + 1) * 128] = jnp.where(spot == mark, 1.0, 0.0).astype(BF)
        for m in range(HALF // 2):
            mark = jnp.where(
                small, heads[2 * m][1:2] + EX * 2 * m, heads[2 * m + 1][1:2] + EX * (2 * m + 1)
            )
            at = HALF * 128 + m * 128
            dst[:, at : at + 128] = jnp.where(spot == mark, 1.0, 0.0).astype(BF)

    def take_across():
        for e in range(2):
            for d in range(HALF):
                at = e * HALF + lax.rem(px + d, HALF)
                if d or e:
                    arrived(across.at[at], across_r.at[at])
                else:

                    @pl.when(jnp.logical_not(home))
                    def _():
                        arrived(across.at[at], across_r.at[at])

        for e in range(2):
            for j in range(HALF):
                x = across[e * HALF + j, HEAD:]
                place(cu.at[e], j, jnp.where(left, x, none))
                place(cv.at[e], j, jnp.where(left, none, x))
        onehot(ohc, [across.at[j] for j in range(HALF)])

    def take_along(s):
        arrived(mine.at[s], along_r.at[s])
        share(s)

    def strip(unit):
        for s in unit:
            arrived(along.at[1, s], sib_r.at[s])
        rows = [jnp.concatenate([along[e, s, HEAD:] for s in unit], axis=0) for e in range(2)]
        t = None
        for c in range(GTOK // 256):
            at = slice(c * 256, (c + 1) * 256)
            pairs = [dot_t(rows[e], cu[e, at]) * dot_t(rows[e], cv[e, at]) for e in range(2)]
            hi, lo = split(pairs[0] + pairs[1])
            mark = ohc[:, at]
            step = dot_t(hi, mark) + dot_t(lo, mark)
            t = step if t is None else t + step
        for i, s in enumerate(unit):
            marks = along[0, s, 0:HEAD].astype(F32)
            mark = jnp.concatenate([marks[0:1], marks[1:2, 0 : TOK - 128]], axis=1)
            mark = jnp.where(line48 == mark, 1.0, 0.0).astype(BF)
            hi, lo = split(t[i * TOK : (i + 1) * TOK])
            tile[s] = dot_n(mark, hi) + dot_n(mark, lo)

    def deliver(unit):
        for s in unit:
            d = (s - 1) % SIDE
            both = tile[s]
            size = jnp.abs(both)
            top = jnp.max(size, axis=(0, 1), keepdims=True)
            power = jnp.ceil(jnp.log2(jnp.maximum(top, 1e-30)) + 1e-4)
            code = (jnp.sqrt(size * jnp.exp2(-power)) * CODE + 0.5).astype(jnp.int32)
            code = jnp.where(both < 0, -code, code)
            word = code[0 : EX // 2] * 65536 + (code[EX // 2 :] & 65535)
            note = jnp.broadcast_to(power.astype(jnp.int32), (8, 128 - 2 * EX))
            for x in range(HALF):
                w = word[:, x * EX : (x + 1) * EX]
                stage[s, x, 0:8] = jnp.concatenate([w[0:8], w[8:16], note], axis=1)
                stage[s, x, 8:12] = jnp.concatenate([w[16:20], w[20:24], note[0:4]], axis=1)
            to = (1 - d) % SIDE
            for k in (2, 1, 3, 0):
                x = lax.rem(pair + k, HALF)
                if k == 0 and d == 0:
                    red[pair, to] = stage[s, x]
                else:
                    sem = red_r.at[pair, to]
                    send(stage.at[s, x], red.at[pair, to], red_s.at[s, k], sem, owner(k, d))

    arrived(mine.at[7], along_r.at[7])
    pass_on(7, 6, 1, 6, (0, HEAD + TOK))
    pass_on(7, 5, 2, 5, (0, HEAD + TOK // 2))
    share(7)
    arrived(mine.at[3], along_r.at[3])
    pass_on(3, 4, 7, 4, (0, HEAD + TOK))
    pass_on(3, 5, 6, 8, (HEAD + TOK // 2, TOK // 2))
    share(3)
    take_along(0)
    take_along(2)
    take_across()
    strip(UNITS[0])
    take_along(4)
    take_along(6)
    arrived(mine.at[5, 0 : HEAD + TOK // 2], along_r.at[5])
    arrived(mine.at[5, HEAD + TOK // 2 :], along_r.at[8])
    share(5)
    pl.semaphore_wait(ready, HALF - 1)
    deliver(UNITS[0])
    for unit in UNITS[1:]:
        strip(unit)
        deliver(unit)

    for s in (1, 2, 0, 7, 3, 5, 6, 4):
        sums = []
        for k in range(HALF):
            y = lax.rem(pair + k, HALF)
            if k or s != 1:
                arrived(red.at[y, s], red_r.at[y, s])
        for y in range(HALF):
            word = red[y, s]
            scale = jnp.exp2(word[:, 2 * EX : 2 * EX + 1].astype(F32)) * (1.0 / (CODE * CODE))
            for half in (word >> 16, (word << 16) >> 16):
                code = half.astype(F32)
                sums.append(code * jnp.abs(code) * scale)
        at = slice(s * EX, (s + 1) * EX)
        for h in range(2):
            part = (sums[h] + sums[2 + h]) + (sums[4 + h] + sums[6 + h])
            base = h * (EX // 2)
            acc[base : base + 8, at] = part[0:8, 0:EX]
            acc[base + 8 : base + 16, at] = part[0:8, EX : 2 * EX]
            acc[base + 16 : base + 20, at] = part[8:12, 0:EX]
            acc[base + 20 : base + 24, at] = part[8:12, EX : 2 * EX]
    out[...] = pltpu.roll(acc[...], lax.rem(q + SIDE - 1, SIDE) * EX, 1)

    for copy in sent:
        copy.wait_send()

    @pl.when(jnp.logical_not(home))
    def _():
        to_core.wait_send()


def per_device(acts, out_grads, proj_in, proj_out, segment_ids):
    kin, depth = proj_in.shape[1:]
    kout, width = proj_out.shape[1:]
    layers = lax.axis_size("layer")
    sem = pltpu.SemaphoreType.DMA
    total = pl.pallas_call(
        kernel,
        name="tile",
        out_shape=jax.ShapeDtypeStruct((EX, SIDE * EX), F32),
        in_specs=[pl.BlockSpec(memory_space=pl.ANY)] * 5,
        out_specs=pl.BlockSpec(memory_space=pltpu.VMEM),
        scratch_shapes=[
            pltpu.VMEM((TOK, depth), BF),
            pltpu.VMEM((TOK, width), BF),
            pltpu.VMEM((kin, depth), BF),
            pltpu.VMEM((kout, width), BF),
            pltpu.VMEM((1, TOK), jnp.int32),
            pltpu.VMEM((SIDE, HEAD + TOK, kin + kout), BF),
            pltpu.VMEM((2, SIDE, HEAD + TOK, kin + kout), BF),
            pltpu.VMEM((2, GTOK, kin + kout), BF),
            pltpu.VMEM((2, GTOK, kin + kout), BF),
            pltpu.VMEM((GEX, GTOK), BF),
            pltpu.VMEM((SIDE, EX, GEX), F32),
            pltpu.VMEM((SIDE, HALF, EX // 4, 128), jnp.int32),
            pltpu.VMEM((HALF, SIDE, EX // 4, 128), jnp.int32),
            pltpu.VMEM((EX, SIDE * EX), F32),
            sem((2 * CHUNKS + 3,)),
            sem((SIDE,)),
            sem((SIDE,)),
            sem((2 * SIDE + 1,)),
            sem((SIDE + 1,)),
            sem((SIDE,)),
            sem((SIDE,)),
            sem((SIDE, HALF)),
            sem((HALF, SIDE)),
            pltpu.SemaphoreType.REGULAR,
        ],
        compiler_params=pltpu.CompilerParams(
            collective_id=0, has_side_effects=True, vmem_limit_bytes=60 << 20
        ),
    )(acts, out_grads, proj_in, proj_out, segment_ids)
    return total * (1.0 / (2 * layers * kin * kout))


def solution(mesh):
    in_specs = (
        P("layer", "ex", None),
        P("layer", "ex", None),
        P("layer", None, None),
        P("layer", None, None),
        P("ex", None),
    )
    out_specs = P("ex", "layer")
    return jax.shard_map(
        per_device, mesh=mesh, in_specs=in_specs, out_specs=out_specs, check_vma=False
    )
```

```python
import jax
import jax.numpy as jnp
from jax import lax
from jax.experimental import pallas as pl
from jax.experimental.pallas import tpu as pltpu
from jax.sharding import PartitionSpec as P

MESH = pl.DeviceIdType.MESH
BF = jnp.bfloat16
F32 = jnp.float32

EX = 48
TOK = 192
SIDE = 8
HALF = SIDE // 2
HEAD = 16
GTOK = HALF * TOK
GEX = HALF * EX
UNITS = ((1, 0, 2, 3, 7), (5, 4, 6))
CODE = 32767.0
CHUNKS = 4


def dot_t(a, b):
    return lax.dot_general(a, b, (((1,), (1,)), ((), ())), preferred_element_type=F32)


def dot_n(a, b):
    return lax.dot_general(a, b, (((1,), (0,)), ((), ())), preferred_element_type=F32)


def split(x):
    hi = x.astype(BF)
    return hi, (x - hi.astype(F32)).astype(BF)


def kernel(
    acts, outg, pin, pout, seg, out,
    ab, gb, pib, pob, segb,
    across, along, cu, cv, ohc, tile, stage, red, acc,
    in_sem, across_s, across_r, along_s, along_r, sib_s, sib_r, red_s, red_r, ready,
):
    layer = lax.axis_index("layer")
    ex = lax.axis_index("ex")
    core = lax.rem(layer, 2)
    pair = layer // 2
    p = ex // SIDE
    q = lax.rem(ex, SIDE)
    kin = pin.shape[1]
    depth = acts.shape[2]
    piece = depth // CHUNKS

    loads = []

    def load(src, dst):
        copy = pltpu.make_async_copy(src, dst, in_sem.at[len(loads)])
        copy.start()
        loads.append(copy)

    load(seg, segb)
    load(pout.at[0], pob)
    load(outg.at[0], gb)
    for k in range(CHUNKS):
        at = pl.ds(k * piece, piece)
        load(pin.at[0, :, at], pib.at[:, at])
        load(acts.at[0, :, at], ab.at[:, at])

    px, py = p // 2, lax.rem(p, 2)
    home = py == core

    def across_to(d, e):
        return (2 * pair + py, (2 * lax.rem(px + d, HALF) + lax.rem(py + e, 2)) * SIDE + q)

    def across_from(d, e):
        return (2 * pair + lax.rem(core + e, 2), (2 * lax.rem(px + d, HALF) + core) * SIDE + q)

    def along_device(d):
        return (layer, p * SIDE + lax.rem(q + d, SIDE))

    other = (layer + 1 - 2 * core, ex)

    def owner(k, d):
        return (2 * lax.rem(pair + k, HALF) + core, p * SIDE + lax.rem(q + d, SIDE))

    barrier = pltpu.get_barrier_semaphore()
    def signal(device):
        pl.semaphore_signal(barrier, inc=1, device_id=device, device_id_type=MESH)

    for d in range(1, SIDE):
        signal(along_device(d))
    signal(other)
    for e in range(2):
        for d in range(HALF):
            if d or e:
                signal(across_from(d, e))

    @pl.when(jnp.logical_not(home))
    def _():
        signal(across_from(0, 0))

    for k in range(1, HALF):
        signal(owner(k, 0))
    greeted = (SIDE - 1) + 1 + SIDE + (HALF - 1) - home.astype(jnp.int32)

    loads[0].wait()
    labels = segb[...].astype(F32)
    tail = labels[:, 128:TOK]
    low = labels[:, 0:128]
    line = lax.broadcasted_iota(jnp.int32, (HEAD, 128), 0)
    head = jnp.where(line == 0, low, jnp.concatenate([tail, tail], axis=1)).astype(BF)
    loads[1].wait()
    loads[2].wait()
    along[0, 1, 0:HEAD] = head
    u = dot_t(gb[...], pob[...])
    v = jnp.zeros((TOK, kin), F32)
    for k in range(CHUNKS):
        loads[3 + 2 * k].wait()
        loads[4 + 2 * k].wait()
        at = pl.ds(k * piece, piece)
        v = v + dot_t(ab[:, at], pib[:, at])
    own = jnp.concatenate([u, v], axis=1).astype(BF)
    along[0, 1, HEAD:] = own
    pl.semaphore_wait(barrier, greeted)
    for k in range(1, HALF):
        pl.semaphore_signal(ready, inc=1, device_id=owner(k, 0), device_id_type=MESH)

    sent = []

    def send(src, dst, send_sem, recv_sem, device):
        copy = pltpu.make_async_remote_copy(
            src, dst, send_sem, recv_sem, device_id=device, device_id_type=MESH
        )
        copy.start()
        sent.append(copy)

    mine = along.at[0]
    to_across = HALF * lax.rem(core + py, 2) + px

    def send_across(d, e):
        sem = across_s.at[HALF * e + d]
        send(mine.at[1], across.at[to_across], sem, across_r.at[to_across], across_to(d, e))

    def send_along(d):
        to = (1 - d) % SIDE
        send(mine.at[1], mine.at[to], along_s.at[d], along_r.at[to], along_device(d))

    def pass_on(src, to, d, sem, at):
        rows = pl.ds(*at)
        send(
            mine.at[src, rows], mine.at[to, rows], along_s.at[sem + SIDE], along_r.at[sem],
            along_device(d),
        )

    def share(s):
        send(mine.at[s], along.at[1, s], sib_s.at[s], sib_r.at[s], other)

    for d in (2, 1, 3, 0):
        send_across(d, 1)
    for d in (2, 6):
        send_along(d)
    for d in (2, 1, 3):
        send_across(d, 0)
    for d in (1, 7):
        send_along(d)
    share(1)
    to_core = pltpu.make_async_remote_copy(
        mine.at[1], across.at[to_across], across_s.at[0], across_r.at[to_across],
        device_id=other, device_id_type=MESH,
    )

    @pl.when(home)
    def _():
        across[px] = along[0, 1]

    @pl.when(jnp.logical_not(home))
    def _():
        to_core.start()

    def arrived(dst, sem):
        pltpu.make_async_remote_copy(
            dst, dst, sib_s.at[0], sem, device_id=other, device_id_type=MESH
        ).wait_recv()

    lane = lax.broadcasted_iota(jnp.int32, (TOK, 128), 1)
    left = lane < kin
    small = lax.broadcasted_iota(jnp.int32, (1, 128), 1) < TOK - 128
    spot = lax.broadcasted_iota(jnp.int32, (GEX, 128), 0).astype(F32)
    none = jnp.zeros((), BF)
    line48 = lax.broadcasted_iota(jnp.int32, (EX, TOK), 0).astype(F32)

    def place(dst, j, x):
        dst[j * 128 : (j + 1) * 128] = x[0:128]
        dst[HALF * 128 + j * 64 : HALF * 128 + (j + 1) * 64] = x[128:TOK]

    def onehot(dst, blocks):
        heads = [b[0:HEAD].astype(F32) for b in blocks]
        for j in range(HALF):
            mark = heads[j][0:1] + EX * j
            dst[:, j * 128 : (j + 1) * 128] = jnp.where(spot == mark, 1.0, 0.0).astype(BF)
        for m in range(HALF // 2):
            mark = jnp.where(
                small, heads[2 * m][1:2] + EX * 2 * m, heads[2 * m + 1][1:2] + EX * (2 * m + 1)
            )
            at = HALF * 128 + m * 128
            dst[:, at : at + 128] = jnp.where(spot == mark, 1.0, 0.0).astype(BF)

    def take_across():
        for e in range(2):
            for d in range(HALF):
                at = e * HALF + lax.rem(px + d, HALF)
                if d or e:
                    arrived(across.at[at], across_r.at[at])
                else:

                    @pl.when(jnp.logical_not(home))
                    def _():
                        arrived(across.at[at], across_r.at[at])

        for e in range(2):
            for j in range(HALF):
                x = across[e * HALF + j, HEAD:]
                place(cu.at[e], j, jnp.where(left, x, none))
                place(cv.at[e], j, jnp.where(left, none, x))
        onehot(ohc, [across.at[j] for j in range(HALF)])

    def take_along(s):
        arrived(mine.at[s], along_r.at[s])
        share(s)

    def strip(unit):
        for s in unit:
            arrived(along.at[1, s], sib_r.at[s])
        rows = [jnp.concatenate([along[e, s, HEAD:] for s in unit], axis=0) for e in range(2)]
        t = None
        for c in range(GTOK // 256):
            at = slice(c * 256, (c + 1) * 256)
            pairs = [dot_t(rows[e], cu[e, at]) * dot_t(rows[e], cv[e, at]) for e in range(2)]
            hi, lo = split(pairs[0] + pairs[1])
            mark = ohc[:, at]
            step = dot_t(hi, mark) + dot_t(lo, mark)
            t = step if t is None else t + step
        for i, s in enumerate(unit):
            marks = along[0, s, 0:HEAD].astype(F32)
            mark = jnp.concatenate([marks[0:1], marks[1:2, 0 : TOK - 128]], axis=1)
            mark = jnp.where(line48 == mark, 1.0, 0.0).astype(BF)
            hi, lo = split(t[i * TOK : (i + 1) * TOK])
            tile[s] = dot_n(mark, hi) + dot_n(mark, lo)

    def deliver(unit):
        for s in unit:
            d = (s - 1) % SIDE
            both = tile[s]
            size = jnp.abs(both)
            top = jnp.max(size, axis=(0, 1), keepdims=True)
            power = jnp.ceil(jnp.log2(jnp.maximum(top, 1e-30)) + 1e-4)
            code = (jnp.sqrt(size * jnp.exp2(-power)) * CODE + 0.5).astype(jnp.int32)
            code = jnp.where(both < 0, -code, code)
            word = code[0 : EX // 2] * 65536 + (code[EX // 2 :] & 65535)
            note = jnp.broadcast_to(power.astype(jnp.int32), (8, 128 - 2 * EX))
            for x in range(HALF):
                w = word[:, x * EX : (x + 1) * EX]
                stage[s, x, 0:8] = jnp.concatenate([w[0:8], w[8:16], note], axis=1)
                stage[s, x, 8:12] = jnp.concatenate([w[16:20], w[20:24], note[0:4]], axis=1)
            to = (1 - d) % SIDE
            for k in (2, 1, 3, 0):
                x = lax.rem(pair + k, HALF)
                if k == 0 and d == 0:
                    red[pair, to] = stage[s, x]
                else:
                    sem = red_r.at[pair, to]
                    send(stage.at[s, x], red.at[pair, to], red_s.at[s, k], sem, owner(k, d))

    arrived(mine.at[7], along_r.at[7])
    pass_on(7, 6, 1, 6, (0, HEAD + TOK))
    pass_on(7, 5, 2, 5, (0, HEAD + TOK // 2))
    arrived(mine.at[3], along_r.at[3])
    pass_on(3, 4, 7, 4, (0, HEAD + TOK))
    pass_on(3, 5, 6, 8, (HEAD + TOK // 2, TOK // 2))
    share(7)
    share(3)
    take_along(0)
    take_along(2)
    take_across()
    strip(UNITS[0])
    take_along(4)
    take_along(6)
    arrived(mine.at[5, 0 : HEAD + TOK // 2], along_r.at[5])
    arrived(mine.at[5, HEAD + TOK // 2 :], along_r.at[8])
    share(5)
    pl.semaphore_wait(ready, HALF - 1)
    deliver(UNITS[0])
    for unit in UNITS[1:]:
        strip(unit)
        deliver(unit)

    for s in (1, 2, 0, 7, 3, 5, 6, 4):
        sums = []
        for k in range(HALF):
            y = lax.rem(pair + k, HALF)
            if k or s != 1:
                arrived(red.at[y, s], red_r.at[y, s])
        for y in range(HALF):
            word = red[y, s]
            scale = jnp.exp2(word[:, 2 * EX : 2 * EX + 1].astype(F32)) * (1.0 / (CODE * CODE))
            for half in (word >> 16, (word << 16) >> 16):
                code = half.astype(F32)
                sums.append(code * jnp.abs(code) * scale)
        at = slice(s * EX, (s + 1) * EX)
        for h in range(2):
            part = (sums[h] + sums[2 + h]) + (sums[4 + h] + sums[6 + h])
            base = h * (EX // 2)
            acc[base : base + 8, at] = part[0:8, 0:EX]
            acc[base + 8 : base + 16, at] = part[0:8, EX : 2 * EX]
            acc[base + 16 : base + 20, at] = part[8:12, 0:EX]
            acc[base + 20 : base + 24, at] = part[8:12, EX : 2 * EX]
    out[...] = pltpu.roll(acc[...], lax.rem(q + SIDE - 1, SIDE) * EX, 1)

    for copy in sent:
        copy.wait_send()

    @pl.when(jnp.logical_not(home))
    def _():
        to_core.wait_send()


def per_device(acts, out_grads, proj_in, proj_out, segment_ids):
    kin, depth = proj_in.shape[1:]
    kout, width = proj_out.shape[1:]
    layers = lax.axis_size("layer")
    sem = pltpu.SemaphoreType.DMA
    total = pl.pallas_call(
        kernel,
        name="tile",
        out_shape=jax.ShapeDtypeStruct((EX, SIDE * EX), F32),
        in_specs=[pl.BlockSpec(memory_space=pl.ANY)] * 5,
        out_specs=pl.BlockSpec(memory_space=pltpu.VMEM),
        scratch_shapes=[
            pltpu.VMEM((TOK, depth), BF),
            pltpu.VMEM((TOK, width), BF),
            pltpu.VMEM((kin, depth), BF),
            pltpu.VMEM((kout, width), BF),
            pltpu.VMEM((1, TOK), jnp.int32),
            pltpu.VMEM((SIDE, HEAD + TOK, kin + kout), BF),
            pltpu.VMEM((2, SIDE, HEAD + TOK, kin + kout), BF),
            pltpu.VMEM((2, GTOK, kin + kout), BF),
            pltpu.VMEM((2, GTOK, kin + kout), BF),
            pltpu.VMEM((GEX, GTOK), BF),
            pltpu.VMEM((SIDE, EX, GEX), F32),
            pltpu.VMEM((SIDE, HALF, EX // 4, 128), jnp.int32),
            pltpu.VMEM((HALF, SIDE, EX // 4, 128), jnp.int32),
            pltpu.VMEM((EX, SIDE * EX), F32),
            sem((2 * CHUNKS + 3,)),
            sem((SIDE,)),
            sem((SIDE,)),
            sem((2 * SIDE + 1,)),
            sem((SIDE + 1,)),
            sem((SIDE,)),
            sem((SIDE,)),
            sem((SIDE, HALF)),
            sem((HALF, SIDE)),
            pltpu.SemaphoreType.REGULAR,
        ],
        compiler_params=pltpu.CompilerParams(
            collective_id=0, has_side_effects=True, vmem_limit_bytes=60 << 20
        ),
    )(acts, out_grads, proj_in, proj_out, segment_ids)
    return total * (1.0 / (2 * layers * kin * kout))


def solution(mesh):
    in_specs = (
        P("layer", "ex", None),
        P("layer", "ex", None),
        P("layer", None, None),
        P("layer", None, None),
        P("ex", None),
    )
    out_specs = P("ex", "layer")
    return jax.shard_map(
        per_device, mesh=mesh, in_specs=in_specs, out_specs=out_specs, check_vma=False
    )
```

```python
import jax
import jax.numpy as jnp
from jax import lax
from jax.experimental import pallas as pl
from jax.experimental.pallas import tpu as pltpu
from jax.sharding import PartitionSpec as P

MESH = pl.DeviceIdType.MESH
BF = jnp.bfloat16
F32 = jnp.float32

EX = 48
TOK = 192
SIDE = 8
HALF = SIDE // 2
HEAD = 16
GTOK = HALF * TOK
GEX = HALF * EX
UNITS = ((1, 0, 2, 3, 7), (5, 4, 6))
CODE = 32767.0
CHUNKS = 4


def dot_t(a, b):
    return lax.dot_general(a, b, (((1,), (1,)), ((), ())), preferred_element_type=F32)


def dot_n(a, b):
    return lax.dot_general(a, b, (((1,), (0,)), ((), ())), preferred_element_type=F32)


def split(x):
    hi = x.astype(BF)
    return hi, (x - hi.astype(F32)).astype(BF)


def kernel(
    acts, outg, pin, pout, seg, out,
    ab, gb, pib, pob, segb,
    across, along, cu, cv, ohc, tile, stage, red, acc,
    in_sem, across_s, across_r, along_s, along_r, sib_s, sib_r, red_s, red_r, ready,
):
    layer = lax.axis_index("layer")
    ex = lax.axis_index("ex")
    core = lax.rem(layer, 2)
    pair = layer // 2
    p = ex // SIDE
    q = lax.rem(ex, SIDE)
    kin = pin.shape[1]
    depth = acts.shape[2]
    piece = depth // CHUNKS

    loads = []

    def load(src, dst):
        copy = pltpu.make_async_copy(src, dst, in_sem.at[len(loads)])
        copy.start()
        loads.append(copy)

    load(seg, segb)
    load(pout.at[0], pob)
    load(outg.at[0], gb)
    for k in range(CHUNKS):
        at = pl.ds(k * piece, piece)
        load(pin.at[0, :, at], pib.at[:, at])
        load(acts.at[0, :, at], ab.at[:, at])

    px, py = p // 2, lax.rem(p, 2)
    home = py == core

    def across_to(d, e):
        return (2 * pair + py, (2 * lax.rem(px + d, HALF) + lax.rem(py + e, 2)) * SIDE + q)

    def across_from(d, e):
        return (2 * pair + lax.rem(core + e, 2), (2 * lax.rem(px + d, HALF) + core) * SIDE + q)

    def along_device(d):
        return (layer, p * SIDE + lax.rem(q + d, SIDE))

    other = (layer + 1 - 2 * core, ex)

    def owner(k, d):
        return (2 * lax.rem(pair + k, HALF) + core, p * SIDE + lax.rem(q + d, SIDE))

    barrier = pltpu.get_barrier_semaphore()
    def signal(device):
        pl.semaphore_signal(barrier, inc=1, device_id=device, device_id_type=MESH)

    for d in range(1, SIDE):
        signal(along_device(d))
    signal(other)
    for e in range(2):
        for d in range(HALF):
            if d or e:
                signal(across_from(d, e))

    @pl.when(jnp.logical_not(home))
    def _():
        signal(across_from(0, 0))

    for k in range(1, HALF):
        signal(owner(k, 0))
    greeted = (SIDE - 1) + 1 + SIDE + (HALF - 1) - home.astype(jnp.int32)

    loads[0].wait()
    labels = segb[...].astype(F32)
    tail = labels[:, 128:TOK]
    low = labels[:, 0:128]
    line = lax.broadcasted_iota(jnp.int32, (HEAD, 128), 0)
    head = jnp.where(line == 0, low, jnp.concatenate([tail, tail], axis=1)).astype(BF)
    loads[1].wait()
    loads[2].wait()
    along[0, 1, 0:HEAD] = head
    u = dot_t(gb[...], pob[...])
    v = jnp.zeros((TOK, kin), F32)
    for k in range(CHUNKS):
        loads[3 + 2 * k].wait()
        loads[4 + 2 * k].wait()
        at = pl.ds(k * piece, piece)
        v = v + dot_t(ab[:, at], pib[:, at])
    own = jnp.concatenate([u, v], axis=1).astype(BF)
    along[0, 1, HEAD:] = own
    pl.semaphore_wait(barrier, greeted)
    for k in range(1, HALF):
        pl.semaphore_signal(ready, inc=1, device_id=owner(k, 0), device_id_type=MESH)

    sent = []

    def send(src, dst, send_sem, recv_sem, device):
        copy = pltpu.make_async_remote_copy(
            src, dst, send_sem, recv_sem, device_id=device, device_id_type=MESH
        )
        copy.start()
        sent.append(copy)

    mine = along.at[0]
    to_across = HALF * lax.rem(core + py, 2) + px

    def send_across(d, e):
        sem = across_s.at[HALF * e + d]
        send(mine.at[1], across.at[to_across], sem, across_r.at[to_across], across_to(d, e))

    def send_along(d):
        to = (1 - d) % SIDE
        send(mine.at[1], mine.at[to], along_s.at[d], along_r.at[to], along_device(d))

    def pass_on(src, to, d, sem, at):
        rows = pl.ds(*at)
        send(
            mine.at[src, rows], mine.at[to, rows], along_s.at[sem + SIDE], along_r.at[sem],
            along_device(d),
        )

    def share(s):
        send(mine.at[s], along.at[1, s], sib_s.at[s], sib_r.at[s], other)

    for d in (2, 1, 3, 0):
        send_across(d, 1)
    first, rest = (0, HEAD + TOK // 2), (HEAD + TOK // 2, TOK // 2)
    for at, parts in ((first, ((2, 2, 7), (6, 6, 3))), (rest, ((2, 21, 9), (6, 22, 10)))):
        for d, sem, got in parts:
            rows = pl.ds(*at)
            to = mine.at[(1 - d) % SIDE, rows]
            send(mine.at[1, rows], to, along_s.at[sem], along_r.at[got], along_device(d))
    for d in (2, 1, 3):
        send_across(d, 0)
    for d in (1, 7):
        send_along(d)
    share(1)
    to_core = pltpu.make_async_remote_copy(
        mine.at[1], across.at[to_across], across_s.at[0], across_r.at[to_across],
        device_id=other, device_id_type=MESH,
    )

    @pl.when(home)
    def _():
        across[px] = along[0, 1]

    @pl.when(jnp.logical_not(home))
    def _():
        to_core.start()

    def arrived(dst, sem):
        pltpu.make_async_remote_copy(
            dst, dst, sib_s.at[0], sem, device_id=other, device_id_type=MESH
        ).wait_recv()

    lane = lax.broadcasted_iota(jnp.int32, (TOK, 128), 1)
    left = lane < kin
    small = lax.broadcasted_iota(jnp.int32, (1, 128), 1) < TOK - 128
    spot = lax.broadcasted_iota(jnp.int32, (GEX, 128), 0).astype(F32)
    none = jnp.zeros((), BF)
    line48 = lax.broadcasted_iota(jnp.int32, (EX, TOK), 0).astype(F32)

    def place(dst, j, x):
        dst[j * 128 : (j + 1) * 128] = x[0:128]
        dst[HALF * 128 + j * 64 : HALF * 128 + (j + 1) * 64] = x[128:TOK]

    def onehot(dst, blocks):
        heads = [b[0:HEAD].astype(F32) for b in blocks]
        for j in range(HALF):
            mark = heads[j][0:1] + EX * j
            dst[:, j * 128 : (j + 1) * 128] = jnp.where(spot == mark, 1.0, 0.0).astype(BF)
        for m in range(HALF // 2):
            mark = jnp.where(
                small, heads[2 * m][1:2] + EX * 2 * m, heads[2 * m + 1][1:2] + EX * (2 * m + 1)
            )
            at = HALF * 128 + m * 128
            dst[:, at : at + 128] = jnp.where(spot == mark, 1.0, 0.0).astype(BF)

    def take_across():
        for e in range(2):
            for d in range(HALF):
                at = e * HALF + lax.rem(px + d, HALF)
                if d or e:
                    arrived(across.at[at], across_r.at[at])
                else:

                    @pl.when(jnp.logical_not(home))
                    def _():
                        arrived(across.at[at], across_r.at[at])

        for e in range(2):
            for j in range(HALF):
                x = across[e * HALF + j, HEAD:]
                place(cu.at[e], j, jnp.where(left, x, none))
                place(cv.at[e], j, jnp.where(left, none, x))
        onehot(ohc, [across.at[j] for j in range(HALF)])

    def take_along(s):
        arrived(mine.at[s], along_r.at[s])
        share(s)

    def strip(unit):
        for s in unit:
            arrived(along.at[1, s], sib_r.at[s])
        rows = [jnp.concatenate([along[e, s, HEAD:] for s in unit], axis=0) for e in range(2)]
        t = None
        for c in range(GTOK // 256):
            at = slice(c * 256, (c + 1) * 256)
            pairs = [dot_t(rows[e], cu[e, at]) * dot_t(rows[e], cv[e, at]) for e in range(2)]
            hi, lo = split(pairs[0] + pairs[1])
            mark = ohc[:, at]
            step = dot_t(hi, mark) + dot_t(lo, mark)
            t = step if t is None else t + step
        for i, s in enumerate(unit):
            marks = along[0, s, 0:HEAD].astype(F32)
            mark = jnp.concatenate([marks[0:1], marks[1:2, 0 : TOK - 128]], axis=1)
            mark = jnp.where(line48 == mark, 1.0, 0.0).astype(BF)
            hi, lo = split(t[i * TOK : (i + 1) * TOK])
            tile[s] = dot_n(mark, hi) + dot_n(mark, lo)

    def deliver(unit):
        for s in unit:
            d = (s - 1) % SIDE
            both = tile[s]
            size = jnp.abs(both)
            top = jnp.max(size, axis=(0, 1), keepdims=True)
            power = jnp.ceil(jnp.log2(jnp.maximum(top, 1e-30)) + 1e-4)
            code = (jnp.sqrt(size * jnp.exp2(-power)) * CODE + 0.5).astype(jnp.int32)
            code = jnp.where(both < 0, -code, code)
            word = code[0 : EX // 2] * 65536 + (code[EX // 2 :] & 65535)
            note = jnp.broadcast_to(power.astype(jnp.int32), (8, 128 - 2 * EX))
            for x in range(HALF):
                w = word[:, x * EX : (x + 1) * EX]
                stage[s, x, 0:8] = jnp.concatenate([w[0:8], w[8:16], note], axis=1)
                stage[s, x, 8:12] = jnp.concatenate([w[16:20], w[20:24], note[0:4]], axis=1)
            to = (1 - d) % SIDE
            for k in (2, 1, 3, 0):
                x = lax.rem(pair + k, HALF)
                if k == 0 and d == 0:
                    red[pair, to] = stage[s, x]
                else:
                    sem = red_r.at[pair, to]
                    send(stage.at[s, x], red.at[pair, to], red_s.at[s, k], sem, owner(k, d))

    arrived(mine.at[7, pl.ds(*first)], along_r.at[7])
    pass_on(7, 6, 1, 6, first)
    pass_on(7, 5, 2, 5, first)
    arrived(mine.at[3, pl.ds(*first)], along_r.at[3])
    pass_on(3, 4, 7, 4, first)
    arrived(mine.at[7, pl.ds(*rest)], along_r.at[9])
    pass_on(7, 6, 1, 11, rest)
    arrived(mine.at[3, pl.ds(*rest)], along_r.at[10])
    pass_on(3, 4, 7, 12, rest)
    pass_on(3, 5, 6, 8, rest)
    share(7)
    share(3)
    take_along(0)
    take_along(2)
    take_across()
    strip(UNITS[0])
    for s, got in ((4, 12), (6, 11)):
        arrived(mine.at[s, pl.ds(*first)], along_r.at[s])
        arrived(mine.at[s, pl.ds(*rest)], along_r.at[got])
        share(s)
    arrived(mine.at[5, 0 : HEAD + TOK // 2], along_r.at[5])
    arrived(mine.at[5, HEAD + TOK // 2 :], along_r.at[8])
    share(5)
    pl.semaphore_wait(ready, HALF - 1)
    deliver(UNITS[0])
    for unit in UNITS[1:]:
        strip(unit)
        deliver(unit)

    for s in (1, 2, 0, 7, 3, 5, 6, 4):
        sums = []
        for k in range(HALF):
            y = lax.rem(pair + k, HALF)
            if k or s != 1:
                arrived(red.at[y, s], red_r.at[y, s])
        for y in range(HALF):
            word = red[y, s]
            scale = jnp.exp2(word[:, 2 * EX : 2 * EX + 1].astype(F32)) * (1.0 / (CODE * CODE))
            for half in (word >> 16, (word << 16) >> 16):
                code = half.astype(F32)
                sums.append(code * jnp.abs(code) * scale)
        at = slice(s * EX, (s + 1) * EX)
        for h in range(2):
            part = (sums[h] + sums[2 + h]) + (sums[4 + h] + sums[6 + h])
            base = h * (EX // 2)
            acc[base : base + 8, at] = part[0:8, 0:EX]
            acc[base + 8 : base + 16, at] = part[0:8, EX : 2 * EX]
            acc[base + 16 : base + 20, at] = part[8:12, 0:EX]
            acc[base + 20 : base + 24, at] = part[8:12, EX : 2 * EX]
    out[...] = pltpu.roll(acc[...], lax.rem(q + SIDE - 1, SIDE) * EX, 1)

    for copy in sent:
        copy.wait_send()

    @pl.when(jnp.logical_not(home))
    def _():
        to_core.wait_send()


def per_device(acts, out_grads, proj_in, proj_out, segment_ids):
    kin, depth = proj_in.shape[1:]
    kout, width = proj_out.shape[1:]
    layers = lax.axis_size("layer")
    sem = pltpu.SemaphoreType.DMA
    total = pl.pallas_call(
        kernel,
        name="tile",
        out_shape=jax.ShapeDtypeStruct((EX, SIDE * EX), F32),
        in_specs=[pl.BlockSpec(memory_space=pl.ANY)] * 5,
        out_specs=pl.BlockSpec(memory_space=pltpu.VMEM),
        scratch_shapes=[
            pltpu.VMEM((TOK, depth), BF),
            pltpu.VMEM((TOK, width), BF),
            pltpu.VMEM((kin, depth), BF),
            pltpu.VMEM((kout, width), BF),
            pltpu.VMEM((1, TOK), jnp.int32),
            pltpu.VMEM((SIDE, HEAD + TOK, kin + kout), BF),
            pltpu.VMEM((2, SIDE, HEAD + TOK, kin + kout), BF),
            pltpu.VMEM((2, GTOK, kin + kout), BF),
            pltpu.VMEM((2, GTOK, kin + kout), BF),
            pltpu.VMEM((GEX, GTOK), BF),
            pltpu.VMEM((SIDE, EX, GEX), F32),
            pltpu.VMEM((SIDE, HALF, EX // 4, 128), jnp.int32),
            pltpu.VMEM((HALF, SIDE, EX // 4, 128), jnp.int32),
            pltpu.VMEM((EX, SIDE * EX), F32),
            sem((2 * CHUNKS + 3,)),
            sem((SIDE,)),
            sem((SIDE,)),
            sem((23,)),
            sem((13,)),
            sem((SIDE,)),
            sem((SIDE,)),
            sem((SIDE, HALF)),
            sem((HALF, SIDE)),
            pltpu.SemaphoreType.REGULAR,
        ],
        compiler_params=pltpu.CompilerParams(
            collective_id=0, has_side_effects=True, vmem_limit_bytes=60 << 20
        ),
    )(acts, out_grads, proj_in, proj_out, segment_ids)
    return total * (1.0 / (2 * layers * kin * kout))


def solution(mesh):
    in_specs = (
        P("layer", "ex", None),
        P("layer", "ex", None),
        P("layer", None, None),
        P("layer", None, None),
        P("ex", None),
    )
    out_specs = P("ex", "layer")
    return jax.shard_map(
        per_device, mesh=mesh, in_specs=in_specs, out_specs=out_specs, check_vma=False
    )
```
